256 devices in a mesh: dp: 4 (over y), seq: 64 (over z, x, core).
Axes of the slice: x: 4, y: 4, z: 8, core: 2. Of those that a mesh axis runs over, the one named last changes fastest.
Arguments:
- lin_q: bfloat16 [16384, 4096], P(('dp', 'seq')), parts along dimension 0, may hold values from -6 to 6
- lin_k: bfloat16 [16384, 4096], P(('dp', 'seq')), parts along dimension 0, may hold values from -0.59765625 to 0.59765625
- lin_v: bfloat16 [16384, 4096], P(('dp', 'seq')), parts along dimension 0, may hold values from -6 to 6
- log_decay: float32 [16384, 32], P(('dp', 'seq')), parts along dimension 0, may hold values from -1 to 0, as said below
- norm_gain: float32 [4096], replicated, may hold values from 0.1 to 1.9
- soft_q: bfloat16 [16384, 4096], P(('dp', 'seq')), parts along dimension 0, may hold values from -200 to 200
- soft_k: bfloat16 [16384, 512], P(('dp', 'seq')), parts along dimension 0, may hold values from -6 to 6
- soft_v: bfloat16 [16384, 512], P(('dp', 'seq')), parts along dimension 0, may hold values from -6 to 6
Outputs:
- lin_out: bfloat16 [16384, 4096], P(('dp', 'seq')), parts along dimension 0
- soft_out: bfloat16 [16384, 4096], P(('dp', 'seq')), parts along dimension 0
The draws below stay inside these ranges and needn't reach their ends.
There are 4 independent parts, one for each index of `dp`. The reference program is written for one: setup_inputs(seed, part) draws one part's arguments, and reference() takes and returns one part's arrays. A program takes and returns all parts, laid end to end along the dimension named above; an argument that names none is the same for every part. Nothing has to cross between parts.
Inputs may be any that keep to these rules, and one draw needn't show every extreme that they name: `log_decay`: non-positive logarithms of decay factors.
All inputs are finite; a program needn't handle non-finite values.
Results may differ from the reference program's by a relative error of at most 0.01195.
Values may be sent and summed in bfloat16 or wider, within the bound.
No kernel may reach another device: no remote copies, remote signals or barrier semaphores. Data moves between devices by JAX's collectives and lax.ppermute only.
A program may use at most 384 MiB of HBM per device.

```python
import jax
import jax.numpy as jnp
from jax import lax

E = 128
LH = 32
QH = 32
KH = 4
TOK_DEV = 64
STREAM_LENGTH = 4096
N_SEQ = 64


def draw_log_decay(key, part):
    fading_speed_seed, brisk_draw_seed, crude_draw_seed, spike_draw_seed, layered_draw_seed = jax.random.split(key, 5)
    fast_rate = jnp.exp(jax.random.uniform(fading_speed_seed, (LH,), jnp.float32, jnp.log(1.0 / 50.0), jnp.log(1.0 / 30.0)))
    slow_rate = jnp.exp(jax.random.uniform(jax.random.fold_in(fading_speed_seed, 7), (LH,), jnp.float32, jnp.log(0.1), 0.0)) * 0.7 / STREAM_LENGTH
    share = 0.5
    fast = jax.random.uniform(brisk_draw_seed, (LH,), jnp.float32) < share
    rate = jnp.where(fast, fast_rate, slow_rate)
    rough = jnp.exp(jax.random.uniform(crude_draw_seed, (STREAM_LENGTH, LH), jnp.float32, jnp.log(0.5), jnp.log(2.0)))
    accelerator_spots = jax.random.randint(spike_draw_seed, (3,), 0, STREAM_LENGTH)
    hit = jnp.any(jnp.arange(STREAM_LENGTH)[:, None] == accelerator_spots[None, :], axis=1)
    depth = jnp.log(jax.random.uniform(layered_draw_seed, (STREAM_LENGTH, LH), jnp.float32, 0.5, 0.8))
    return -rate[None, :] * rough + jnp.where(hit[:, None], depth, 0.0)


def query_key_pair(key):
    k_keys = jax.random.fold_in(key, 11)
    k_queries = jax.random.fold_in(key, 12)
    keys = jnp.clip(jax.random.normal(k_keys, (STREAM_LENGTH, KH, E), jnp.float32), -6.0, 6.0)
    queries = jnp.clip(jax.random.normal(k_queries, (STREAM_LENGTH, QH, E), jnp.float32), -6.0, 6.0)
    return (queries.reshape(STREAM_LENGTH, QH * E), keys.reshape(STREAM_LENGTH, KH * E))


def draw_soft_q(key, part):
    return query_key_pair(key)[0].astype(jnp.bfloat16)


def draw_soft_k(key, part):
    return query_key_pair(key)[1].astype(jnp.bfloat16)


def steps_of(rng, extent, pieces, least, largest):
    level = 1.0
    for position, parts in pieces:
        heights = jax.random.uniform(jax.random.fold_in(jax.random.fold_in(rng, 6), position), (parts,), jnp.float32, least / len(pieces), largest / len(pieces))
        level = level * jnp.repeat(jnp.exp(heights), extent[position] // parts).reshape((-1,) + (1,) * (len(extent) - 1 - position))
    return level


def gaussian(key, shape, scale, bound, shards=(), kind=jnp.bfloat16):
    values = scale * jax.random.normal(key, shape, jnp.float32)
    if shards:
        values = values * steps_of(key, shape, shards, -0.22, 0.18)
    return jnp.clip(values, -bound, bound).astype(kind)


def setup_inputs(seed: int = 0, part: int = 0) -> dict:
    arg_keys = jax.random.split(jax.random.key(seed), 9)
    own_keys = jax.random.split(jax.random.fold_in(arg_keys[8], part), 9)
    lin_q = gaussian(own_keys[0], (STREAM_LENGTH, LH * E), 1.0, 6.0, ((0, 64),))
    lin_k = gaussian(own_keys[1], (STREAM_LENGTH, LH * E), 0.088, 0.59765625, ((0, 64),))
    lin_v = gaussian(own_keys[2], (STREAM_LENGTH, LH * E), 1.0, 6.0, ((0, 64),))
    log_decay = draw_log_decay(jax.random.fold_in(jax.random.fold_in(arg_keys[8], part), 71), part)
    norm_gain = jnp.clip(1.0 + 0.18 * jax.random.normal(arg_keys[4], (LH * E,), jnp.float32), 0.1, 1.9)
    soft_q = draw_soft_q(jax.random.fold_in(jax.random.fold_in(arg_keys[8], part), 71), part)
    soft_k = draw_soft_k(jax.random.fold_in(jax.random.fold_in(arg_keys[8], part), 71), part)
    soft_v = gaussian(own_keys[7], (STREAM_LENGTH, KH * E), 1.0, 6.0, ((0, 64),))
    return {"lin_q": lin_q, "lin_k": lin_k, "lin_v": lin_v, "log_decay": log_decay, "norm_gain": norm_gain, "soft_q": soft_q, "soft_k": soft_k, "soft_v": soft_v}


def slab_linear(state_in, slab):
    q_slab, k_slab, v_slab, a_slab = slab
    rows = q_slab.shape[0]
    q3 = q_slab.reshape(rows, LH, E)
    k3 = k_slab.reshape(rows, LH, E)
    v3 = v_slab.reshape(rows, LH, E)
    cum = jnp.cumsum(a_slab, axis=0)
    scores = jnp.einsum('thd,shd->hts', q3.astype(jnp.float32), k3.astype(jnp.float32))
    diff = cum.T[:, :, None] - cum.T[:, None, :]
    causal = jnp.arange(rows)[:, None] >= jnp.arange(rows)[None, :]
    weights = jnp.where(causal[None], jnp.exp(jnp.where(causal[None], diff, 0.0)), 0.0)
    intra_w = (scores * weights).astype(jnp.bfloat16)
    intra = jnp.einsum('hts,shd->thd', intra_w.astype(jnp.float32), v3.astype(jnp.float32))
    qdec = q3.astype(jnp.float32) * jnp.exp(cum)[:, :, None]
    cross = jnp.einsum('thd,hde->the', qdec, state_in, precision=lax.Precision.HIGHEST)
    total = (intra + cross).reshape(rows, LH * E)
    last = cum[-1]
    kw = k3.astype(jnp.float32) * jnp.exp(last[None, :] - cum)[:, :, None]
    contrib = jnp.einsum('thd,the->hde', kw, v3.astype(jnp.float32), precision=lax.Precision.HIGHEST)
    state_out = jnp.exp(last)[:, None, None] * state_in + contrib
    return (state_out, total)

def reference(lin_q, lin_k, lin_v, log_decay, norm_gain, soft_q, soft_k, soft_v):
    slabs = (lin_q.reshape(N_SEQ, TOK_DEV, LH * E), lin_k.reshape(N_SEQ, TOK_DEV, LH * E), lin_v.reshape(N_SEQ, TOK_DEV, LH * E), log_decay.reshape(N_SEQ, TOK_DEV, LH))
    start = jnp.zeros((LH, E, E), jnp.float32)
    unused, totals = lax.scan(slab_linear, start, slabs)
    total = totals.reshape(STREAM_LENGTH, LH * E)
    rms = jnp.sqrt(lax.optimization_barrier(jnp.mean(total * total, axis=1, keepdims=True)) + 1e-06)
    lin_out = (total / rms * norm_gain[None, :]).astype(jnp.bfloat16)
    group = QH // KH
    block = min(STREAM_LENGTH, 512)
    q_heads = soft_q.reshape(STREAM_LENGTH, QH, E).transpose(1, 0, 2)
    k_heads = soft_k.reshape(STREAM_LENGTH, KH, E).transpose(1, 0, 2)
    v_heads = soft_v.reshape(STREAM_LENGTH, KH, E).transpose(1, 0, 2)
    key_pos = jnp.arange(STREAM_LENGTH)

    def one_head(head):
        q_h = q_heads[head]
        k_h = k_heads[head // group]
        v_h = v_heads[head // group]

        def one_block(first):
            q_b = lax.dynamic_slice_in_dim(q_h, first, block, 0)
            s = jnp.dot(q_b, k_h.T, preferred_element_type=jnp.float32) / jnp.sqrt(jnp.float32(E))
            qpos = first + jnp.arange(block)
            mask = key_pos[None, :] <= qpos[:, None]
            s = jnp.where(mask, s, jnp.float32(-1e+30))
            m = lax.optimization_barrier(jnp.max(s, axis=1, keepdims=True))
            p = jnp.where(mask, jnp.exp(s - m), 0.0)
            denom = lax.optimization_barrier(jnp.sum(p, axis=1, keepdims=True))
            out = jnp.dot(p.astype(jnp.bfloat16), v_h, preferred_element_type=jnp.float32)
            return out / denom
        firsts = (jnp.arange(STREAM_LENGTH // block) * block).astype(jnp.int32)
        return lax.map(one_block, firsts).reshape(STREAM_LENGTH, E)
    outs = lax.map(one_head, jnp.arange(QH))
    soft_out = outs.transpose(1, 0, 2).reshape(STREAM_LENGTH, QH * E).astype(jnp.bfloat16)
    return (lin_out, soft_out)
```

```python
import functools

import jax
import jax.numpy as jnp
from jax import lax
from jax.experimental import pallas as pl
from jax.experimental.pallas import tpu as pltpu
from jax.sharding import PartitionSpec as P

SIZE = 128
F32 = jnp.float32
BF16 = jnp.bfloat16
VMEM_LIMIT = 48 * 1024 * 1024
EXTRA = 16


def params():
    return pltpu.CompilerParams(vmem_limit_bytes=VMEM_LIMIT)


def running_sum(log_decay):
    rows = log_decay.shape[0]
    t = lax.broadcasted_iota(jnp.int32, (rows, rows), 0)
    s = lax.broadcasted_iota(jnp.int32, (rows, rows), 1)
    lower = jnp.where(s <= t, 1.0, 0.0).astype(F32)
    return jnp.dot(lower, log_decay, precision=lax.Precision.HIGHEST, preferred_element_type=F32)


def running_sum_rows(log_decay):
    rows = log_decay.shape[0]
    s = lax.broadcasted_iota(jnp.int32, (rows, rows), 0)
    t = lax.broadcasted_iota(jnp.int32, (rows, rows), 1)
    upper = jnp.where(s <= t, 1.0, 0.0).astype(F32)
    return lax.dot_general(
        log_decay,
        upper,
        (((0,), (0,)), ((), ())),
        precision=lax.Precision.HIGHEST,
        preferred_element_type=F32,
    )


def contrib_kernel(k_ref, v_ref, decay_ref, out_ref):
    heads = decay_ref.shape[1]
    half = SIZE // 2
    cum = running_sum(decay_ref[...])
    last = cum[-1:, :]
    to_end = jnp.exp(last - cum)
    row = lax.broadcasted_iota(jnp.int32, (EXTRA, SIZE), 0)
    for h in range(heads):
        cols = slice(h * SIZE, (h + 1) * SIZE)
        kw = (k_ref[:, cols].astype(F32) * to_end[:, h : h + 1]).astype(BF16)
        state = lax.dot_general(
            kw, v_ref[:, cols], (((0,), (0,)), ((), ())), preferred_element_type=F32
        ).astype(BF16)
        total = jnp.broadcast_to(last[:, h : h + 1], (EXTRA, SIZE))
        high = total.astype(BF16).astype(F32)
        mid = (total - high).astype(BF16).astype(F32)
        low = total - high - mid
        terms = jnp.where(row == 0, high, jnp.where(row == 1, mid, jnp.where(row == 2, low, 0.0)))
        terms = terms.astype(BF16)
        for part in range(2):
            out_ref[2 * h + part, :half, :] = state[part * half : (part + 1) * half]
            out_ref[2 * h + part, half:, :] = terms


def contributions(k, v, log_decay):
    heads = log_decay.shape[1]
    return pl.pallas_call(
        contrib_kernel,
        out_shape=jax.ShapeDtypeStruct((2 * heads, SIZE // 2 + EXTRA, SIZE), BF16),
        compiler_params=params(),
    )(k, v, log_decay)


def scan_kernel(in_ref, out_ref):
    slabs = in_ref.shape[0]
    half = SIZE // 2

    def step(n, state):
        out_ref[n] = state.astype(BF16)
        terms = in_ref[n, half:, :].astype(F32)
        gain = jnp.exp(jnp.sum(terms, axis=0, keepdims=True))
        return state * gain + in_ref[n, :half, :].astype(F32)

    lax.fori_loop(0, slabs, step, jnp.zeros((half, SIZE), F32), unroll=4)


def scan_states(parts):
    return pl.pallas_call(
        scan_kernel,
        out_shape=jax.ShapeDtypeStruct((parts.shape[0], SIZE // 2, SIZE), BF16),
        compiler_params=params(),
    )(parts)


def intra_kernel(q_ref, k_ref, v_ref, decay_ref, out_ref):
    rows, heads = decay_ref.shape
    cum = running_sum(decay_ref[...])
    cum_rows = running_sum_rows(decay_ref[...])
    t = lax.broadcasted_iota(jnp.int32, (rows, rows), 0)
    s = lax.broadcasted_iota(jnp.int32, (rows, rows), 1)
    causal = s <= t
    for h in range(heads):
        cols = slice(h * SIZE, (h + 1) * SIZE)
        score = lax.dot_general(
            q_ref[:, cols], k_ref[:, cols], (((1,), (1,)), ((), ())), preferred_element_type=F32
        )
        diff = jnp.where(causal, cum[:, h : h + 1] - cum_rows[h : h + 1, :], 0.0)
        weight = jnp.where(causal, score * jnp.exp(diff), 0.0).astype(BF16)
        out_ref[:, cols] = jnp.dot(weight, v_ref[:, cols], preferred_element_type=F32)


def intra_part(q, k, v, log_decay):
    return pl.pallas_call(
        intra_kernel,
        out_shape=jax.ShapeDtypeStruct(q.shape, F32),
        compiler_params=params(),
    )(q, k, v, log_decay)


def final_kernel(q_ref, intra_ref, state_ref, decay_ref, gain_ref, out_ref, total_ref):
    rows, heads = decay_ref.shape
    grown = jnp.exp(running_sum(decay_ref[...]))
    square = jnp.zeros((rows, SIZE), F32)
    for h in range(heads):
        cols = slice(h * SIZE, (h + 1) * SIZE)
        cross = jnp.dot(q_ref[:, cols], state_ref[h], preferred_element_type=F32)
        total = intra_ref[:, cols] + grown[:, h : h + 1] * cross
        total_ref[:, cols] = total
        square += total * total
    mean = jnp.sum(square, axis=1, keepdims=True) / (heads * SIZE)
    scale = lax.rsqrt(mean + 1e-06)
    for h in range(heads):
        cols = slice(h * SIZE, (h + 1) * SIZE)
        out_ref[:, cols] = (total_ref[:, cols] * scale * gain_ref[:, cols]).astype(BF16)


def final_part(q, intra, state, log_decay, gain):
    return pl.pallas_call(
        final_kernel,
        out_shape=jax.ShapeDtypeStruct(q.shape, BF16),
        scratch_shapes=[pltpu.VMEM(q.shape, F32)],
        compiler_params=params(),
    )(q, intra, state, log_decay, gain)


LOG2E = 1.4426950408889634


def flash_kernel(block, base_ref, q_ref, k_ref, v_ref, out_ref, rows_ref):
    tokens = q_ref.shape[0]
    group = q_ref.shape[1] // SIZE
    base = base_ref[0]
    for h in range(group):
        rows_ref[h * tokens : (h + 1) * tokens, :] = q_ref[:, h * SIZE : (h + 1) * SIZE]
    q = rows_ref[...]
    width = group * tokens
    scale = LOG2E / (SIZE**0.5)

    def visit(start, carry, masked):
        top, norm, accum = carry
        k = k_ref[pl.ds(start, block), :]
        v = v_ref[pl.ds(start, block), :]
        s = lax.dot_general(k, q, (((1,), (1,)), ((), ())), preferred_element_type=F32) * scale
        if masked:
            key = start + lax.broadcasted_iota(jnp.int32, s.shape, 0)
            token = base + lax.rem(lax.broadcasted_iota(jnp.int32, s.shape, 1), tokens)
            s = jnp.where(key <= token, s, -1e30)
        new_top = jnp.maximum(top, jnp.max(s, axis=0, keepdims=True))
        shrink = jnp.exp2(top - new_top)
        p = jnp.exp2(s - new_top)
        norm = norm * shrink + jnp.sum(p, axis=0, keepdims=True)
        got = lax.dot_general(
            v, p.astype(BF16), (((0,), (0,)), ((), ())), preferred_element_type=F32
        )
        return new_top, norm, accum * shrink + got

    full = lax.div(base, block)
    carry = (
        jnp.full((1, width), -1e30, F32),
        jnp.zeros((1, width), F32),
        jnp.zeros((SIZE, width), F32),
    )
    carry = visit(pl.multiple_of(full * block, block), carry, True)
    top, norm, accum = lax.fori_loop(
        0, full, lambda i, c: visit(pl.multiple_of(i * block, block), c, False), carry
    )
    out = jnp.transpose(accum / norm).astype(BF16)
    for h in range(group):
        out_ref[:, h * SIZE : (h + 1) * SIZE] = out[h * tokens : (h + 1) * tokens]


def flash(q, kv, base, block=512):
    tokens = q.shape[0]
    kv_heads = kv.shape[1] // (2 * SIZE)
    width = q.shape[1] // kv_heads
    keys = kv.shape[0]
    return pl.pallas_call(
        functools.partial(flash_kernel, block),
        out_shape=jax.ShapeDtypeStruct(q.shape, BF16),
        grid_spec=pltpu.PrefetchScalarGridSpec(
            num_scalar_prefetch=1,
            grid=(kv_heads,),
            in_specs=[
                pl.BlockSpec((tokens, width), lambda g, b: (0, g)),
                pl.BlockSpec((keys, SIZE), lambda g, b: (0, g)),
                pl.BlockSpec((keys, SIZE), lambda g, b: (0, kv_heads + g)),
            ],
            out_specs=pl.BlockSpec((tokens, width), lambda g, b: (0, g)),
            scratch_shapes=[pltpu.VMEM((width // SIZE * tokens, SIZE), BF16)],
        ),
        compiler_params=params(),
    )(base, q, kv, kv)


def on_device(lin_q, lin_k, lin_v, log_decay, norm_gain, soft_q, soft_k, soft_v):
    tokens = lin_q.shape[0]
    heads = log_decay.shape[1]
    base = (lax.axis_index("seq") * tokens).astype(jnp.int32).reshape(1)
    with jax.named_scope("keys_values"):
        kv = lax.all_gather(jnp.concatenate([soft_k, soft_v], axis=1), "seq", axis=0, tiled=True)
    with jax.named_scope("states"):
        parts = contributions(lin_k, lin_v, log_decay)
        parts = lax.all_to_all(parts, "seq", 0, 0)
        intra = intra_part(lin_q, lin_k, lin_v, log_decay)
        states = scan_states(parts)
        states = lax.all_to_all(states, "seq", 0, 0).reshape(heads, SIZE, SIZE)
        lin_out = final_part(lin_q, intra, states, log_decay, norm_gain.reshape(1, -1))
    with jax.named_scope("softmax"):
        soft_out = flash(soft_q, kv, base)
    return lin_out, soft_out


def solution(mesh):
    split = P(("dp", "seq"), None)
    in_specs = (split,) * 4 + (P(),) + (split,) * 3
    return jax.shard_map(
        on_device, mesh=mesh, in_specs=in_specs, out_specs=(split, split), check_vma=False
    )
```

```python
import functools

import jax
import jax.numpy as jnp
from jax import lax
from jax.experimental import pallas as pl
from jax.experimental.pallas import tpu as pltpu
from jax.sharding import PartitionSpec as P

SIZE = 128
F32 = jnp.float32
BF16 = jnp.bfloat16
VMEM_LIMIT = 48 * 1024 * 1024


def params():
    return pltpu.CompilerParams(vmem_limit_bytes=VMEM_LIMIT)


def running_sum(log_decay):
    rows = log_decay.shape[0]
    t = lax.broadcasted_iota(jnp.int32, (rows, rows), 0)
    s = lax.broadcasted_iota(jnp.int32, (rows, rows), 1)
    lower = jnp.where(s <= t, 1.0, 0.0).astype(F32)
    return jnp.dot(lower, log_decay, precision=lax.Precision.HIGHEST, preferred_element_type=F32)


def running_sum_rows(log_decay):
    rows = log_decay.shape[0]
    s = lax.broadcasted_iota(jnp.int32, (rows, rows), 0)
    t = lax.broadcasted_iota(jnp.int32, (rows, rows), 1)
    upper = jnp.where(s <= t, 1.0, 0.0).astype(F32)
    return lax.dot_general(
        log_decay,
        upper,
        (((0,), (0,)), ((), ())),
        precision=lax.Precision.HIGHEST,
        preferred_element_type=F32,
    )


def contrib_kernel(c_ref, k_ref, v_ref, decay_ref, keep_ref, send_ref):
    heads = decay_ref.shape[1]
    half = SIZE // 2
    cum = running_sum(decay_ref[...])
    to_end = jnp.exp(cum[-1:, :] - cum)
    first = c_ref[0] == 0
    for h in range(heads):
        cols = slice(h * SIZE, (h + 1) * SIZE)
        kw = (k_ref[:, cols].astype(F32) * to_end[:, h : h + 1]).astype(BF16)
        state = lax.dot_general(
            kw, v_ref[:, cols], (((0,), (0,)), ((), ())), preferred_element_type=F32
        )
        upper, lower = state[:half], state[half:]
        keep_ref[h] = jnp.where(first, upper, lower).astype(BF16)
        send_ref[h] = jnp.where(first, lower, upper).astype(BF16)


def sums_by_head(decay):
    ones = jnp.ones((decay.shape[0], SIZE), F32)
    return lax.dot_general(
        decay,
        ones,
        (((0,), (0,)), ((), ())),
        precision=lax.Precision.HIGHEST,
        preferred_element_type=F32,
    )


def in_terms(total):
    high = total.astype(BF16).astype(F32)
    mid = (total - high).astype(BF16).astype(F32)
    return jnp.concatenate([high, mid, total - high - mid, jnp.zeros_like(total)], axis=0).astype(BF16)


def from_terms(terms, n):
    terms = terms.astype(F32)
    return terms[:n] + terms[n : 2 * n] + terms[2 * n : 3 * n]


def chip_kernel(x_ref, c_ref, decay_ref, other_ref, keep_ref, came_ref, *refs):
    outs, (gain_ref, both_ref) = refs[:N_X], refs[N_X:]
    heads = decay_ref.shape[1] // N_X
    half = SIZE // 2
    mine = sums_by_head(decay_ref[...])
    other = sums_by_head(other_ref[...])
    first = c_ref[0] == 0
    gain = jnp.exp(jnp.where(first, other, mine))
    gain_ref[0] = jnp.where(first, gain, 1.0)
    gain_ref[1] = jnp.where(first, 1.0, gain)
    both_ref[...] = mine + other
    for k, out in enumerate(outs):
        head = lax.rem(x_ref[0] + k, N_X) * heads
        for h in range(heads):
            row = pl.ds(head + h, 1)
            state = (
                keep_ref[head + h].astype(F32) * gain_ref[0, row, :]
                + came_ref[head + h].astype(F32) * gain_ref[1, row, :]
            )
            out[h * half : (h + 1) * half, :] = state.astype(BF16)
        out[heads * half :, :] = in_terms(both_ref[pl.ds(pl.multiple_of(head, heads), heads), :])


def group_kernel(x_ref, *refs):
    came, (out, order) = refs[:N_X], refs[N_X:]
    rows = out.shape[0]
    half = SIZE // 2
    heads = rows // (half + 4)
    for k, ref in enumerate(came):
        order[lax.rem(x_ref[0] - k + N_X, N_X)] = ref[...]
    sums = [from_terms(order[p, heads * half :, :], heads) for p in range(N_X)]
    gains = [jnp.exp(a) for a in sums]
    for h in range(heads):
        span = slice(h * half, (h + 1) * half)
        state = order[0, span, :].astype(F32)
        for p in range(1, N_X):
            state = state * gains[p][h : h + 1] + order[p, span, :].astype(F32)
        out[span, :] = state.astype(BF16)
    out[heads * half :, :] = in_terms(sum(sums[1:], sums[0]))


def enter_kernel(x_ref, z_ref, order, *refs):
    groups, outs, states = refs[: N_Z - 1], refs[N_Z - 1 : -1], refs[-1]
    rows = order.shape[1]
    half = SIZE // 2
    heads = rows // (half + 4)
    gains = [jnp.exp(from_terms(ref[heads * half :, :], heads)) for ref in groups]
    steps = [jnp.exp(from_terms(order[p, heads * half :, :], heads)) for p in range(N_X)]
    for h in range(heads):
        span = slice(h * half, (h + 1) * half)
        head = slice(h, h + 1)
        state = jnp.zeros((half, SIZE), F32)
        for i, ref in enumerate(groups):
            after = state * gains[i][head] + ref[span, :].astype(F32)
            state = jnp.where(z_ref[0] >= N_Z - 1 - i, after, 0.0)
        for p in range(N_X):
            states[p, span, :] = state.astype(BF16)
            state = state * steps[p][head] + order[p, span, :].astype(F32)
    for k, out in enumerate(outs):
        out[...] = states[lax.rem(x_ref[0] - k + N_X, N_X)]


def bridge_kernel(x_ref, c_ref, decay_ref, other_ref, keep_ref, came_ref, *refs):
    entering, (mine_ref, send_ref, gain_ref) = refs[:N_X], refs[N_X:]
    half = SIZE // 2
    heads = entering[0].shape[0] // half
    first = c_ref[0] == 0
    mine = sums_by_head(decay_ref[...])
    other = sums_by_head(other_ref[...])
    gain_ref[...] = jnp.exp(jnp.where(first, mine, other))
    for k, ref in enumerate(entering):
        head = lax.rem(x_ref[0] + k, N_X) * heads
        for h in range(heads):
            state = ref[h * half : (h + 1) * half, :].astype(F32)
            added = jnp.where(first, keep_ref[head + h].astype(F32), came_ref[head + h].astype(F32))
            after = state * gain_ref[pl.ds(head + h, 1), :] + added
            mine_ref[head + h] = jnp.where(first, state, after).astype(BF16)
            send_ref[head + h] = jnp.where(first, after, state).astype(BF16)


def intra_kernel(q_ref, k_ref, v_ref, decay_ref, out_ref):
    rows, heads = decay_ref.shape
    cum = running_sum(decay_ref[...])
    cum_rows = running_sum_rows(decay_ref[...])
    t = lax.broadcasted_iota(jnp.int32, (rows, rows), 0)
    s = lax.broadcasted_iota(jnp.int32, (rows, rows), 1)
    causal = s <= t
    for h in range(heads):
        cols = slice(h * SIZE, (h + 1) * SIZE)
        score = lax.dot_general(
            q_ref[:, cols], k_ref[:, cols], (((1,), (1,)), ((), ())), preferred_element_type=F32
        )
        diff = jnp.where(causal, cum[:, h : h + 1] - cum_rows[h : h + 1, :], 0.0)
        weight = jnp.where(causal, score * jnp.exp(diff), 0.0).astype(BF16)
        out_ref[:, cols] = jnp.dot(weight, v_ref[:, cols], preferred_element_type=F32)


def intra_part(q, k, v, log_decay):
    return pl.pallas_call(
        intra_kernel,
        out_shape=jax.ShapeDtypeStruct(q.shape, F32),
        compiler_params=params(),
    )(q, k, v, log_decay)


def final_kernel(
    c_ref, q_ref, intra_ref, mine_ref, came_ref, decay_ref, gain_ref, out_ref, total_ref, state_ref
):
    rows, heads = decay_ref.shape
    half = SIZE // 2
    grown = jnp.exp(running_sum(decay_ref[...]))
    square = jnp.zeros((rows, SIZE), F32)
    mine = pl.ds(pl.multiple_of(c_ref[0] * half, half), half)
    other = pl.ds(pl.multiple_of((1 - c_ref[0]) * half, half), half)
    state_ref[:, mine, :] = mine_ref[...]
    state_ref[:, other, :] = came_ref[...]
    for h in range(heads):
        cols = slice(h * SIZE, (h + 1) * SIZE)
        cross = jnp.dot(q_ref[:, cols], state_ref[h], preferred_element_type=F32)
        total = intra_ref[:, cols] + grown[:, h : h + 1] * cross
        total_ref[:, cols] = total
        square += total * total
    mean = jnp.sum(square, axis=1, keepdims=True) / (heads * SIZE)
    scale = lax.rsqrt(mean + 1e-06)
    for h in range(heads):
        cols = slice(h * SIZE, (h + 1) * SIZE)
        out_ref[:, cols] = (total_ref[:, cols] * scale * gain_ref[:, cols]).astype(BF16)


LOG2E = 1.4426950408889634
SCALE = LOG2E / SIZE**0.5
N_Z, N_X = 8, 4
HIDDEN = -1e30


def call(kernel, outs, scalars, arrays, scratch=()):
    return pl.pallas_call(
        kernel,
        out_shape=outs,
        in_specs=[pl.BlockSpec(memory_space=pltpu.SMEM)] * len(scalars)
        + [pl.BlockSpec(memory_space=pltpu.VMEM)] * len(arrays),
        scratch_shapes=list(scratch),
        compiler_params=params(),
    )(*scalars, *arrays)


def shape(rows, cols, dtype=BF16):
    return jax.ShapeDtypeStruct((rows, cols), dtype)


def pack_kernel(x_ref, q_ref, k_ref, v_ref, *outs):
    wide = q_ref.shape[1] // N_X
    for k, out in enumerate(outs):
        j = lax.rem(x_ref[0] + k, N_X)
        out[:, :wide] = q_ref[:, pl.ds(pl.multiple_of(j * wide, wide), wide)]
        head = pl.ds(pl.multiple_of(j * SIZE, SIZE), SIZE)
        out[:, wide : wide + SIZE] = k_ref[:, head]
        out[:, wide + SIZE :] = v_ref[:, head]


def share_kernel(c_ref, *refs):
    came, (keep, send, kv) = refs[:N_X], refs[N_X:]
    wide = came[0].shape[1] - 2 * SIZE
    half = wide // 2
    tokens = came[0].shape[0]
    mine = pl.ds(pl.multiple_of(c_ref[0] * half, half), half)
    other = pl.ds(pl.multiple_of((1 - c_ref[0]) * half, half), half)
    for k, ref in enumerate(came):
        rows = slice(k * tokens, (k + 1) * tokens)
        keep[rows, :] = ref[:, mine]
        send[rows, :half] = ref[:, other]
        send[rows, half:] = ref[:, wide:]
        kv[rows, :] = ref[:, wide:]


def group_positions(x, core, shape, axis, tokens):
    i = lax.broadcasted_iota(jnp.int32, shape, axis)
    part = lax.div(i, N_X * tokens)
    k = lax.rem(lax.div(i, tokens), N_X)
    from_x = lax.rem(x - k + N_X, N_X)
    from_core = jnp.where(part == 0, core, 1 - core)
    return (2 * from_x + from_core) * tokens + lax.rem(i, tokens)


def own_kernel(x_ref, c_ref, keep_ref, came_ref, kv_ref, q_ref, top_ref, norm_ref, accum_ref):
    part = keep_ref.shape[0]
    tokens = part // N_X
    heads = keep_ref.shape[1] // SIZE
    wide = heads * SIZE
    key_pos = group_positions(x_ref[0], c_ref[0], (2 * part, 1), 0, tokens)
    q_pos = group_positions(x_ref[0], c_ref[0], (1, 2 * part), 1, tokens)
    seen = key_pos <= q_pos
    k = jnp.concatenate([kv_ref[:, :SIZE], came_ref[:, wide : wide + SIZE]], axis=0)
    v = jnp.concatenate([kv_ref[:, SIZE:], came_ref[:, wide + SIZE :]], axis=0)
    for h in range(heads):
        cols = slice(h * SIZE, (h + 1) * SIZE)
        q = jnp.concatenate([keep_ref[:, cols], came_ref[:, cols]], axis=0)
        q_ref[h] = q
        s = lax.dot_general(k, q, (((1,), (1,)), ((), ())), preferred_element_type=F32)
        s = jnp.where(seen, s * SCALE, HIDDEN)
        top = jnp.max(s, axis=0, keepdims=True)
        p = jnp.exp2(s - top)
        top_ref[h] = top
        norm_ref[h] = jnp.sum(p, axis=0, keepdims=True)
        accum_ref[h] = lax.dot_general(
            v, p.astype(BF16), (((0,), (0,)), ((), ())), preferred_element_type=F32
        )


def visit(q, top, norm, accum, chunks, seen, s_ref):
    rows = chunks[0].shape[0]
    new_top = top
    for i, ref in enumerate(chunks):
        s = lax.dot_general(
            ref[:, :SIZE], q, (((1,), (1,)), ((), ())), preferred_element_type=F32
        )
        s = s * SCALE
        s_ref[i * rows : (i + 1) * rows, :] = s
        here = jnp.max(s, axis=0, keepdims=True)
        new_top = jnp.maximum(new_top, jnp.where(seen[i], here, HIDDEN))
    shrink = jnp.exp2(top - new_top)
    norm = norm * shrink
    accum = accum * shrink
    for i, ref in enumerate(chunks):
        level = jnp.where(seen[i], new_top, -2.0 * HIDDEN)
        p = jnp.exp2(s_ref[i * rows : (i + 1) * rows, :] - level)
        norm = norm + jnp.sum(p, axis=0, keepdims=True)
        accum = accum + lax.dot_general(
            ref[:, SIZE:], p.astype(BF16), (((0,), (0,)), ((), ())), preferred_element_type=F32
        )
    return new_top, norm, accum


def seen_chunks(z, steps):
    return [z - step >= 0 if step > 0 else z - step >= N_Z for step in steps for _ in range(2)]


def near_kernel(steps, z_ref, q_ref, top_ref, norm_ref, accum_ref, *refs):
    count = 2 * len(steps)
    chunks, (new_top, new_norm, new_accum, s_ref) = refs[:count], refs[count:]
    seen = seen_chunks(z_ref[0], steps)
    for h in range(q_ref.shape[0]):
        new_top[h], new_norm[h], new_accum[h] = visit(
            q_ref[h], top_ref[h], norm_ref[h], accum_ref[h], chunks, seen, s_ref
        )


def far_kernel(steps, z_ref, q_ref, top_ref, norm_ref, accum_ref, *refs):
    count = 2 * len(steps)
    chunks, (out_mine, out_other, s_ref) = refs[:count], refs[count:]
    part = out_mine.shape[0]
    seen = seen_chunks(z_ref[0], steps)
    for h in range(q_ref.shape[0]):
        _, norm, accum = visit(
            q_ref[h], top_ref[h], norm_ref[h], accum_ref[h], chunks, seen, s_ref
        )
        out = jnp.transpose(accum / norm).astype(BF16)
        cols = slice(h * SIZE, (h + 1) * SIZE)
        out_mine[:, cols] = out[:part]
        out_other[:, cols] = out[part:]


def merge_kernel(c_ref, mine_ref, came_ref, *outs):
    half = mine_ref.shape[1]
    tokens = outs[0].shape[0]
    mine = pl.ds(pl.multiple_of(c_ref[0] * half, half), half)
    other = pl.ds(pl.multiple_of((1 - c_ref[0]) * half, half), half)
    for k, out in enumerate(outs):
        rows = slice(k * tokens, (k + 1) * tokens)
        out[:, mine] = mine_ref[rows, :]
        out[:, other] = came_ref[rows, :]


def place_kernel(x_ref, *refs):
    came, out = refs[:N_X], refs[N_X]
    wide = came[0].shape[1]
    for k, ref in enumerate(came):
        j = lax.rem(x_ref[0] + k, N_X)
        out[:, pl.ds(pl.multiple_of(j * wide, wide), wide)] = ref[...]


def along_x(a, k):
    return lax.ppermute(a, "x", [(i, (i + k) % N_X) for i in range(N_X)])


def along_z(a, k):
    return lax.ppermute(a, "z", [(i, (i + k) % N_Z) for i in range(N_Z)])


def other_core(a):
    return lax.ppermute(a, "core", [(0, 1), (1, 0)])


def attention_layers(lin_q, lin_k, lin_v, log_decay, norm_gain, soft_q, soft_k, soft_v):
    tokens, lin_heads = log_decay.shape
    rows_half = SIZE // 2
    wide = soft_q.shape[1] // N_X
    half = wide // 2
    heads = half // SIZE
    part = N_X * tokens
    z, x, core = (lax.axis_index(a).astype(jnp.int32).reshape(1) for a in ("z", "x", "core"))
    packed = call(pack_kernel, (shape(tokens, wide + 2 * SIZE),) * N_X, (x,), (soft_q, soft_k, soft_v))
    soft_came = [packed[0]] + [along_x(packed[i], i) for i in range(1, N_X)]
    halves = jax.ShapeDtypeStruct((lin_heads, rows_half, SIZE), BF16)
    decay_other = other_core(log_decay)
    keep, send = call(contrib_kernel, (halves, halves), (core,), (lin_k, lin_v, log_decay))
    state_came = other_core(send)
    of_chip = shape(lin_heads // N_X * (rows_half + 4), SIZE)
    parts = call(
        chip_kernel,
        (of_chip,) * N_X,
        (x, core),
        (log_decay, decay_other, keep, state_came),
        [pltpu.VMEM((2, lin_heads, SIZE), F32), pltpu.VMEM((lin_heads, SIZE), F32)],
    )
    parts = [parts[0]] + [along_x(parts[i], i) for i in range(1, N_X)]
    group, order = call(
        group_kernel, (of_chip, jax.ShapeDtypeStruct((N_X, *of_chip.shape), BF16)), (x,), parts
    )
    q_keep, q_send, kv = call(
        share_kernel,
        (shape(part, half), shape(part, half + 2 * SIZE), shape(part, 2 * SIZE)),
        (core,),
        soft_came,
    )
    q_came = other_core(q_send)
    chunk, groups = {}, {}
    up, down, state_up, state_down = kv, kv, group, group
    for step in range(1, N_Z // 2 + 1):
        up = along_z(up, 1)
        chunk[step] = (up, other_core(up))
        state_up = along_z(state_up, 1)
        groups[step] = state_up
        if step < N_Z // 2:
            down = along_z(down, -1)
            chunk[-step] = (down, other_core(down))
            state_down = along_z(state_down, -1)
            groups[N_Z - step] = state_down
    row = jax.ShapeDtypeStruct((heads, 1, 2 * part), F32)
    held_shape = (row, row, jax.ShapeDtypeStruct((heads, SIZE, 2 * part), F32))
    q, *held = call(
        own_kernel,
        (jax.ShapeDtypeStruct((heads, 2 * part, SIZE), BF16), *held_shape),
        (x, core),
        (q_keep, q_came, kv),
    )
    intra = intra_part(lin_q, lin_k, lin_v, log_decay)
    near, far = (1, -1, 2, -2), (3, -3, 4)
    held = call(
        functools.partial(near_kernel, near),
        held_shape,
        (z,),
        [q, *held] + [a for step in near for a in chunk[step]],
        [pltpu.VMEM((2 * len(near) * part, 2 * part), F32)],
    )
    states = call(
        enter_kernel,
        (shape(lin_heads // N_X * rows_half, SIZE),) * N_X,
        (x, z),
        [order] + [groups[d] for d in range(N_Z - 1, 0, -1)],
        [pltpu.VMEM((N_X, lin_heads // N_X * rows_half, SIZE), BF16)],
    )
    states = [states[0]] + [along_x(states[i], -i) for i in range(1, N_X)]
    out_mine, out_other = call(
        functools.partial(far_kernel, far),
        (shape(part, half),) * 2,
        (z,),
        [q, *held] + [a for step in far for a in chunk[step]],
        [pltpu.VMEM((2 * len(far) * part, 2 * part), F32)],
    )
    out_came = other_core(out_other)
    outs = call(merge_kernel, (shape(tokens, wide),) * N_X, (core,), (out_mine, out_came))
    out_came = [outs[0]] + [along_x(outs[i], -i) for i in range(1, N_X)]
    mine, send = call(
        bridge_kernel,
        (halves, halves),
        (x, core),
        [log_decay, decay_other, keep, state_came, *states],
        [pltpu.VMEM((lin_heads, SIZE), F32)],
    )
    lin_out = call(
        final_kernel,
        shape(tokens, lin_heads * SIZE),
        (core,),
        (lin_q, intra, mine, other_core(send), log_decay, norm_gain.reshape(1, -1)),
        [pltpu.VMEM(lin_q.shape, F32), pltpu.VMEM((lin_heads, SIZE, SIZE), BF16)],
    )
    soft_out = call(place_kernel, shape(tokens, wide * N_X), (x,), out_came)
    return lin_out, soft_out


def solution(mesh):
    grid = mesh.devices.reshape(mesh.devices.shape[0], N_Z, N_X, 2)
    mesh = jax.sharding.Mesh(grid, ("dp", "z", "x", "core"))
    split = P(("dp", "z", "x", "core"), None)
    in_specs = (split,) * 4 + (P(),) + (split,) * 3
    return jax.shard_map(
        attention_layers, mesh=mesh, in_specs=in_specs, out_specs=(split, split), check_vma=False
    )
```

```python
import functools

import jax
import jax.numpy as jnp
from jax import lax
from jax.experimental import pallas as pl
from jax.experimental.pallas import tpu as pltpu
from jax.sharding import PartitionSpec as P

SIZE = 128
F32 = jnp.float32
BF16 = jnp.bfloat16
VMEM_LIMIT = 16 * 1024 * 1024


def params():
    return pltpu.CompilerParams(vmem_limit_bytes=VMEM_LIMIT)


def running_sum(decay):
    rows = decay.shape[1]
    t = lax.broadcasted_iota(jnp.int32, (rows, rows), 0)
    s = lax.broadcasted_iota(jnp.int32, (rows, rows), 1)
    lower = jnp.where(s <= t, 1.0, 0.0).astype(F32)
    return lax.dot_general(
        lower,
        decay,
        (((1,), (1,)), ((), ())),
        precision=lax.Precision.HIGHEST,
        preferred_element_type=F32,
    )


def running_sum_rows(decay):
    rows = decay.shape[1]
    s = lax.broadcasted_iota(jnp.int32, (rows, rows), 0)
    t = lax.broadcasted_iota(jnp.int32, (rows, rows), 1)
    upper = jnp.where(s <= t, 1.0, 0.0).astype(F32)
    return jnp.dot(decay, upper, precision=lax.Precision.HIGHEST, preferred_element_type=F32)


def contrib_kernel(c_ref, k_ref, v_ref, decay_ref, keep_ref, send_ref, sums_ref):
    heads = decay_ref.shape[0]
    half = SIZE // 2
    cum = running_sum(decay_ref[...])
    to_end = jnp.exp(cum[-1:, :] - cum)
    first = c_ref[0] == 0
    for h in range(heads):
        cols = slice(h * SIZE, (h + 1) * SIZE)
        kw = (k_ref[:, cols].astype(F32) * to_end[:, h : h + 1]).astype(BF16)
        state = lax.dot_general(
            kw, v_ref[:, cols], (((0,), (0,)), ((), ())), preferred_element_type=F32
        )
        upper, lower = state[:half], state[half:]
        keep_ref[h] = jnp.where(first, upper, lower).astype(BF16)
        send_ref[h] = jnp.where(first, lower, upper).astype(BF16)
    sums_ref[...] = sums_by_head(decay_ref[...])
    terms = in_terms(sums_ref[...])
    for i in range(terms.shape[0] // half):
        send_ref[heads + i] = terms[i * half : (i + 1) * half]


def other_sums(came_ref, heads):
    terms = [came_ref[i] for i in range(heads, came_ref.shape[0])]
    return from_terms(jnp.concatenate(terms, axis=0), heads)


def sums_by_head(decay):
    ones = jnp.ones((decay.shape[1], SIZE), F32)
    return jnp.dot(decay, ones, precision=lax.Precision.HIGHEST, preferred_element_type=F32)


def in_terms(total):
    high = total.astype(BF16).astype(F32)
    mid = (total - high).astype(BF16).astype(F32)
    return jnp.concatenate([high, mid, total - high - mid, jnp.zeros_like(total)], axis=0).astype(BF16)


def from_terms(terms, n):
    terms = terms.astype(F32)
    return terms[:n] + terms[n : 2 * n] + terms[2 * n : 3 * n]


def chip_kernel(x_ref, c_ref, sums_ref, keep_ref, came_ref, *refs):
    outs, (gain_ref, both_ref) = refs[:N_X], refs[N_X:]
    heads = sums_ref.shape[0] // N_X
    half = SIZE // 2
    mine = sums_ref[...]
    other = other_sums(came_ref, sums_ref.shape[0])
    first = c_ref[0] == 0
    gain = jnp.exp(jnp.where(first, other, mine))
    gain_ref[0] = jnp.where(first, gain, 1.0)
    gain_ref[1] = jnp.where(first, 1.0, gain)
    both_ref[...] = mine + other
    for k, out in enumerate(outs):
        head = lax.rem(x_ref[0] + offset(k, c_ref[0]), N_X) * heads
        for h in range(heads):
            row = pl.ds(head + h, 1)
            state = (
                keep_ref[head + h].astype(F32) * gain_ref[0, row, :]
                + came_ref[head + h].astype(F32) * gain_ref[1, row, :]
            )
            out[h * half : (h + 1) * half, :] = state.astype(BF16)
        out[heads * half :, :] = in_terms(both_ref[pl.ds(pl.multiple_of(head, heads), heads), :])


def group_kernel(x_ref, c_ref, *refs):
    came, (out, order) = refs[:N_X], refs[N_X:]
    rows = out.shape[0]
    half = SIZE // 2
    heads = rows // (half + 4)
    for k, ref in enumerate(came):
        order[lax.rem(x_ref[0] - offset(k, c_ref[0]) + N_X, N_X)] = ref[...]
    sums = [from_terms(order[p, heads * half :, :], heads) for p in range(N_X)]
    gains = [jnp.exp(a) for a in sums]
    for h in range(heads):
        span = slice(h * half, (h + 1) * half)
        state = order[0, span, :].astype(F32)
        for p in range(1, N_X):
            state = state * gains[p][h : h + 1] + order[p, span, :].astype(F32)
        out[span, :] = state.astype(BF16)
    out[heads * half :, :] = in_terms(sum(sums[1:], sums[0]))


def enter_kernel(x_ref, z_ref, c_ref, order, *refs):
    groups, outs, states = refs[: N_Z - 1], refs[N_Z - 1 : -1], refs[-1]
    rows = order.shape[1]
    half = SIZE // 2
    heads = rows // (half + 4)
    gains = [jnp.exp(from_terms(ref[heads * half :, :], heads)) for ref in groups]
    steps = [jnp.exp(from_terms(order[p, heads * half :, :], heads)) for p in range(N_X)]
    for h in range(heads):
        span = slice(h * half, (h + 1) * half)
        head = slice(h, h + 1)
        state = jnp.zeros((half, SIZE), F32)
        for i, ref in enumerate(groups):
            after = state * gains[i][head] + ref[span, :].astype(F32)
            state = jnp.where(z_ref[0] >= N_Z - 1 - i, after, 0.0)
        for p in range(N_X):
            states[p, span, :] = state.astype(BF16)
            state = state * steps[p][head] + order[p, span, :].astype(F32)
    for k, out in enumerate(outs):
        out[...] = states[lax.rem(x_ref[0] - offset(k, c_ref[0]) + N_X, N_X)]


def bridge_kernel(x_ref, c_ref, sums_ref, keep_ref, came_ref, *refs):
    entering, (mine_ref, send_ref, gain_ref) = refs[:N_X], refs[N_X:]
    half = SIZE // 2
    heads = entering[0].shape[0] // half
    first = c_ref[0] == 0
    mine = sums_ref[...]
    other = other_sums(came_ref, sums_ref.shape[0])
    gain_ref[...] = jnp.exp(jnp.where(first, mine, other))
    for k, ref in enumerate(entering):
        head = lax.rem(x_ref[0] + offset(k, c_ref[0]), N_X) * heads
        for h in range(heads):
            state = ref[h * half : (h + 1) * half, :].astype(F32)
            added = jnp.where(first, keep_ref[head + h].astype(F32), came_ref[head + h].astype(F32))
            after = state * gain_ref[pl.ds(head + h, 1), :] + added
            mine_ref[head + h] = jnp.where(first, state, after).astype(BF16)
            send_ref[head + h] = jnp.where(first, after, state).astype(BF16)


def intra_kernel(q_ref, k_ref, v_ref, decay_ref, out_ref):
    heads, rows = decay_ref.shape
    cum = running_sum(decay_ref[...])
    cum_rows = running_sum_rows(decay_ref[...])
    t = lax.broadcasted_iota(jnp.int32, (rows, rows), 0)
    s = lax.broadcasted_iota(jnp.int32, (rows, rows), 1)
    causal = s <= t
    for h in range(heads):
        cols = slice(h * SIZE, (h + 1) * SIZE)
        score = lax.dot_general(
            q_ref[:, cols], k_ref[:, cols], (((1,), (1,)), ((), ())), preferred_element_type=F32
        )
        diff = jnp.where(causal, cum[:, h : h + 1] - cum_rows[h : h + 1, :], 0.0)
        weight = jnp.where(causal, score * jnp.exp(diff), 0.0).astype(BF16)
        out_ref[:, cols] = jnp.dot(weight, v_ref[:, cols], preferred_element_type=F32)


def final_kernel(
    c_ref, q_ref, intra_ref, mine_ref, came_ref, decay_ref, gain_ref, out_ref, total_ref, state_ref
):
    heads, rows = decay_ref.shape
    half = SIZE // 2
    grown = jnp.exp(running_sum(decay_ref[...]))
    square = jnp.zeros((rows, SIZE), F32)
    mine = pl.ds(pl.multiple_of(c_ref[0] * half, half), half)
    other = pl.ds(pl.multiple_of((1 - c_ref[0]) * half, half), half)
    state_ref[:, mine, :] = mine_ref[...]
    state_ref[:, other, :] = came_ref[...]
    for h in range(heads):
        cols = slice(h * SIZE, (h + 1) * SIZE)
        cross = jnp.dot(q_ref[:, cols], state_ref[h], preferred_element_type=F32)
        total = intra_ref[:, cols] + grown[:, h : h + 1] * cross
        total_ref[:, cols] = total
        square += total * total
    mean = jnp.sum(square, axis=1, keepdims=True) / (heads * SIZE)
    scale = lax.rsqrt(mean + 1e-06)
    for h in range(heads):
        cols = slice(h * SIZE, (h + 1) * SIZE)
        out_ref[:, cols] = (total_ref[:, cols] * scale * gain_ref[:, cols]).astype(BF16)


LOG2E = 1.4426950408889634
SCALE = LOG2E / SIZE**0.5
N_Z, N_X = 8, 4
HIDDEN = -1e30


def call(kernel, outs, scalars, arrays, scratch=()):
    name = getattr(kernel, "func", kernel).__name__
    return pl.pallas_call(
        kernel,
        name=name,
        out_shape=outs,
        in_specs=[pl.BlockSpec(memory_space=pltpu.SMEM)] * len(scalars)
        + [pl.BlockSpec(memory_space=pltpu.VMEM)] * len(arrays),
        scratch_shapes=list(scratch),
        compiler_params=params(),
    )(*scalars, *arrays)


def shape(rows, cols, dtype=BF16):
    return jax.ShapeDtypeStruct((rows, cols), dtype)


def offset(k, core):
    one = jnp.where(core == 0, 1, N_X - 1)
    return (0, N_X // 2, one, N_X - one)[k]


def pack_kernel(x_ref, c_ref, q_ref, k_ref, v_ref, *outs):
    wide = q_ref.shape[1] // N_X
    for k, out in enumerate(outs):
        j = lax.rem(x_ref[0] + offset(k, c_ref[0]), N_X)
        out[:, :wide] = q_ref[:, pl.ds(pl.multiple_of(j * wide, wide), wide)]
        head = pl.ds(pl.multiple_of(j * SIZE, SIZE), SIZE)
        out[:, wide : wide + SIZE] = k_ref[:, head]
        out[:, wide + SIZE :] = v_ref[:, head]


def stack_kernel(*refs):
    came, out = refs[:N_X], refs[N_X]
    tokens = came[0].shape[0]
    for k, ref in enumerate(came):
        out[k * tokens : (k + 1) * tokens, :] = ref[...]


def chunk_kernel(c_ref, mine_ref, other_ref, out_ref):
    rows, wide = mine_ref.shape
    out_ref[pl.ds(pl.multiple_of(c_ref[0] * rows, rows), rows), :] = mine_ref[:, wide - 2 * SIZE :]
    out_ref[pl.ds(pl.multiple_of((1 - c_ref[0]) * rows, rows), rows), :] = other_ref[:, wide - 2 * SIZE :]


def group_positions(x, core, shape, axis, tokens):
    i = lax.broadcasted_iota(jnp.int32, shape, axis)
    part = lax.div(i, N_X * tokens)
    k = lax.rem(lax.div(i, tokens), N_X)
    from_core = jnp.where(part == 0, core, 1 - core)
    away = jnp.zeros_like(k)
    for n in range(1, N_X):
        away = jnp.where(k == n, offset(n, from_core), away)
    from_x = lax.rem(x - away + N_X, N_X)
    return (2 * from_x + from_core) * tokens + lax.rem(i, tokens)


def own_kernel(x_ref, c_ref, mine_ref, other_ref, q_ref, top_ref, norm_ref, accum_ref):
    part, wide = mine_ref.shape
    tokens = part // N_X
    heads = wide // SIZE - 2
    key_pos = group_positions(x_ref[0], c_ref[0], (part, 1), 0, tokens)
    q_pos = group_positions(x_ref[0], c_ref[0], (1, 2 * part), 1, tokens)
    seen = key_pos <= q_pos
    k = mine_ref[:, wide - 2 * SIZE : wide - SIZE]
    v = mine_ref[:, wide - SIZE :]
    for h in range(heads):
        cols = slice(h * SIZE, (h + 1) * SIZE)
        q = jnp.concatenate([mine_ref[:, cols], other_ref[:, cols]], axis=0)
        q_ref[h] = q
        s = lax.dot_general(k, q, (((1,), (1,)), ((), ())), preferred_element_type=F32)
        s = jnp.where(seen, s * SCALE, HIDDEN)
        top = jnp.max(s, axis=0, keepdims=True)
        p = jnp.exp2(s - top)
        top_ref[h] = top
        norm_ref[h] = jnp.sum(p, axis=0, keepdims=True)
        accum_ref[h] = lax.dot_general(
            v, p.astype(BF16), (((0,), (0,)), ((), ())), preferred_element_type=F32
        )


def visit(q, top, norm, accum, k, v, seen):
    s = lax.dot_general(k, q, (((1,), (1,)), ((), ())), preferred_element_type=F32) * SCALE
    here = jnp.max(s, axis=0, keepdims=True)
    new_top = jnp.maximum(top, jnp.where(seen, here, HIDDEN))
    shrink = jnp.exp2(top - new_top)
    p = jnp.exp2(s - jnp.where(seen, new_top, -2.0 * HIDDEN))
    norm = norm * shrink + jnp.sum(p, axis=0, keepdims=True)
    accum = accum * shrink + lax.dot_general(
        v, p.astype(BF16), (((0,), (0,)), ((), ())), preferred_element_type=F32
    )
    return new_top, norm, accum


def more_kernel(step, z_ref, c_ref, q_ref, top_ref, norm_ref, accum_ref, chunk_ref, *outs):
    new_top, new_norm, new_accum = outs
    seen = z_ref[0] >= jnp.where(c_ref[0] == 0, step, N_Z - step)
    k, v = chunk_ref[:, :SIZE], chunk_ref[:, SIZE:]
    for h in range(q_ref.shape[0]):
        new_top[h], new_norm[h], new_accum[h] = visit(
            q_ref[h], top_ref[h], norm_ref[h], accum_ref[h], k, v, seen
        )


def last_kernel(z_ref, c_ref, q_ref, top_ref, norm_ref, accum_ref, chunk_ref, mine_ref, send_ref):
    rows = chunk_ref.shape[0] // 2
    part = mine_ref.shape[2]
    here = pl.ds(pl.multiple_of(c_ref[0] * rows, rows), rows)
    k, v = chunk_ref[here, :SIZE], chunk_ref[here, SIZE:]
    for h in range(q_ref.shape[0]):
        top, norm, accum = visit(
            q_ref[h], top_ref[h], norm_ref[h], accum_ref[h], k, v, z_ref[0] >= N_Z // 2
        )
        for out, span in ((mine_ref, slice(0, part)), (send_ref, slice(part, 2 * part))):
            out[h, :SIZE, :] = accum[:, span]
            out[h, SIZE : SIZE + 1, :] = norm[:, span]
            out[h, SIZE + 1 : SIZE + 2, :] = top[:, span]


def join_kernel(mine_ref, came_ref, *outs):
    tokens = outs[0].shape[0]
    for h in range(mine_ref.shape[0]):
        tops = [ref[h, SIZE + 1 : SIZE + 2, :] for ref in (mine_ref, came_ref)]
        top = jnp.maximum(*tops)
        one, two = (jnp.exp2(t - top) for t in tops)
        norm = mine_ref[h, SIZE : SIZE + 1, :] * one + came_ref[h, SIZE : SIZE + 1, :] * two
        accum = mine_ref[h, :SIZE, :] * (one / norm) + came_ref[h, :SIZE, :] * (two / norm)
        out = jnp.transpose(accum).astype(BF16)
        for k, ref in enumerate(outs):
            ref[:, h * SIZE : (h + 1) * SIZE] = out[k * tokens : (k + 1) * tokens]


def place_kernel(x_ref, c_ref, *refs):
    came, out = refs[:N_X], refs[N_X]
    wide = came[0].shape[1]
    for k, ref in enumerate(came):
        j = lax.rem(x_ref[0] + offset(k, c_ref[0]), N_X)
        out[:, pl.ds(pl.multiple_of(j * wide, wide), wide)] = ref[...]


def along_x(a, way):
    steps = (way, -way)
    pairs = [(2 * i + c, 2 * ((i + steps[c]) % N_X) + c) for i in range(N_X) for c in range(2)]
    return lax.ppermute(a, ("x", "core"), pairs)


def to_partners(parts):
    own, opposite, near, far = parts
    return [own, along_x(along_x(opposite, 1), 1), along_x(near, 1), along_x(far, -1)]


def from_partners(parts):
    own, opposite, near, far = parts
    return [own, along_x(opposite, 2), along_x(near, -1), along_x(far, 1)]


def along_z(a, k):
    return lax.ppermute(a, "z", [(i, (i + k) % N_Z) for i in range(N_Z)])


def along_ring(a):
    pairs = [(2 * i + c, 2 * ((i + (1, -1)[c]) % N_Z) + c) for i in range(N_Z) for c in range(2)]
    return lax.ppermute(a, ("z", "core"), pairs)


def other_core(a):
    return lax.ppermute(a, "core", [(0, 1), (1, 0)])


def after(a, *others):
    return lax.optimization_barrier((a, others))[0]


def attention_layers(lin_q, lin_k, lin_v, log_decay, norm_gain, soft_q, soft_k, soft_v):
    tokens, lin_heads = log_decay.shape
    decay = log_decay.T
    rows_half = SIZE // 2
    lin_share = lin_heads // N_X
    wide = soft_q.shape[1] // N_X
    heads = wide // SIZE
    part = N_X * tokens
    z, x, core = (lax.axis_index(a).astype(jnp.int32).reshape(1) for a in ("z", "x", "core"))
    packed = call(pack_kernel, (shape(tokens, wide + 2 * SIZE),) * N_X, (x, core), (soft_q, soft_k, soft_v))
    keep, send, decay_sums = call(
        contrib_kernel,
        (
            jax.ShapeDtypeStruct((lin_heads, rows_half, SIZE), BF16),
            jax.ShapeDtypeStruct((lin_heads + 4 * lin_heads // rows_half, rows_half, SIZE), BF16),
            jax.ShapeDtypeStruct((lin_heads, SIZE), F32),
        ),
        (core,),
        (lin_k, lin_v, decay),
    )
    state_came = other_core(send)
    of_chip = shape(lin_share * (rows_half + 4), SIZE)
    parts = call(
        chip_kernel,
        (of_chip,) * N_X,
        (x, core),
        (decay_sums, keep, state_came),
        [pltpu.VMEM((2, lin_heads, SIZE), F32), pltpu.VMEM((lin_heads, SIZE), F32)],
    )
    intra = call(
        intra_kernel, shape(tokens, lin_heads * SIZE, F32), (), (lin_q, lin_k, lin_v, decay)
    )
    packed = after(packed, parts[0])
    soft_came = to_partners(packed)
    parts_came = to_partners(parts)
    group, order = call(
        group_kernel, (of_chip, jax.ShapeDtypeStruct((N_X, *of_chip.shape), BF16)), (x, core), parts_came
    )
    mine = call(stack_kernel, shape(part, wide + 2 * SIZE), (), after(soft_came, group, intra))
    other = other_core(mine)
    chunk = call(chunk_kernel, shape(2 * part, 2 * SIZE), (core,), (mine, other))
    row = jax.ShapeDtypeStruct((heads, 1, 2 * part), F32)
    held_shape = (row, row, jax.ShapeDtypeStruct((heads, SIZE, 2 * part), F32))
    state_up, state_down, groups = group, group, {}
    for step in range(1, N_Z // 2 + 1):
        state_up = along_z(state_up, 1)
        groups[step] = state_up
        if step < N_Z // 2:
            state_down = along_z(state_down, -1)
            groups[N_Z - step] = state_down
    states = call(
        enter_kernel,
        (shape(lin_share * rows_half, SIZE),) * N_X,
        (x, z, core),
        [order] + [groups[d] for d in range(N_Z - 1, 0, -1)],
        [pltpu.VMEM((N_X, lin_share * rows_half, SIZE), BF16)],
    )
    states = from_partners(states)
    for step in range(1, N_Z // 2 + 1):
        came = along_ring(chunk)
        if step == 1:
            q, *held = call(
                own_kernel,
                (jax.ShapeDtypeStruct((heads, 2 * part, SIZE), BF16), *held_shape),
                (x, core),
                (mine, other),
            )
        else:
            held = call(
                functools.partial(more_kernel, step - 1), held_shape, (z, core), (q, *held, chunk)
            )
        if step < N_Z // 2 - 1:
            ahead = [groups[step + 1]] + ([groups[N_Z - step - 1]] if step + 1 < N_Z // 2 else [])
        else:
            ahead = [] if step < N_Z // 2 else states[1:]
        chunk = after(came, held[0], *ahead)
    sums = jax.ShapeDtypeStruct((heads, SIZE + 8, part), F32)
    sums_mine, sums_send = call(last_kernel, (sums, sums), (z, core), (q, *held, chunk))
    outs = call(
        join_kernel, (shape(tokens, wide),) * N_X, (), (sums_mine, other_core(sums_send))
    )
    outs = from_partners(outs)
    halves = jax.ShapeDtypeStruct((lin_heads, rows_half, SIZE), BF16)
    mine, send = call(
        bridge_kernel,
        (halves, halves),
        (x, core),
        [decay_sums, keep, state_came, *states],
        [pltpu.VMEM((lin_heads, SIZE), F32)],
    )
    lin_out = call(
        final_kernel,
        shape(tokens, lin_heads * SIZE),
        (core,),
        (lin_q, intra, mine, other_core(send), decay, norm_gain.reshape(1, -1)),
        [pltpu.VMEM(lin_q.shape, F32), pltpu.VMEM((lin_heads, SIZE, SIZE), BF16)],
    )
    soft_out = call(place_kernel, shape(tokens, wide * N_X), (x, core), outs)
    return lin_out, soft_out


def solution(mesh):
    grid = mesh.devices.reshape(mesh.devices.shape[0], N_Z, N_X, 2)
    mesh = jax.sharding.Mesh(grid, ("dp", "z", "x", "core"))
    split = P(("dp", "z", "x", "core"), None)
    in_specs = (split,) * 4 + (P(),) + (split,) * 3
    return jax.shard_map(
        attention_layers, mesh=mesh, in_specs=in_specs, out_specs=(split, split), check_vma=False
    )
```

```python
import functools

import jax
import jax.numpy as jnp
from jax import lax
from jax.experimental import pallas as pl
from jax.experimental.pallas import tpu as pltpu
from jax.sharding import PartitionSpec as P

SIZE = 128
F32 = jnp.float32
BF16 = jnp.bfloat16
VMEM_LIMIT = 16 * 1024 * 1024


def params():
    return pltpu.CompilerParams(vmem_limit_bytes=VMEM_LIMIT)


def running_sum(decay):
    rows = decay.shape[1]
    t = lax.broadcasted_iota(jnp.int32, (rows, rows), 0)
    s = lax.broadcasted_iota(jnp.int32, (rows, rows), 1)
    lower = jnp.where(s <= t, 1.0, 0.0).astype(F32)
    return lax.dot_general(
        lower,
        decay,
        (((1,), (1,)), ((), ())),
        precision=lax.Precision.HIGHEST,
        preferred_element_type=F32,
    )


def running_sum_rows(decay):
    rows = decay.shape[1]
    s = lax.broadcasted_iota(jnp.int32, (rows, rows), 0)
    t = lax.broadcasted_iota(jnp.int32, (rows, rows), 1)
    upper = jnp.where(s <= t, 1.0, 0.0).astype(F32)
    return jnp.dot(decay, upper, precision=lax.Precision.HIGHEST, preferred_element_type=F32)


def contrib_kernel(c_ref, k_ref, v_ref, decay_ref, keep_ref, send_ref, sums_ref):
    heads = decay_ref.shape[0]
    half = SIZE // 2
    cum = running_sum(decay_ref[...])
    to_end = jnp.exp(cum[-1:, :] - cum)
    first = c_ref[0] == 0
    for h in range(heads):
        cols = slice(h * SIZE, (h + 1) * SIZE)
        kw = (k_ref[:, cols].astype(F32) * to_end[:, h : h + 1]).astype(BF16)
        state = lax.dot_general(
            kw, v_ref[:, cols], (((0,), (0,)), ((), ())), preferred_element_type=F32
        )
        upper, lower = state[:half], state[half:]
        keep_ref[h] = jnp.where(first, upper, lower).astype(BF16)
        send_ref[h] = jnp.where(first, lower, upper).astype(BF16)
    sums_ref[...] = sums_by_head(decay_ref[...])
    terms = in_terms(sums_ref[...])
    for i in range(terms.shape[0] // half):
        send_ref[heads + i] = terms[i * half : (i + 1) * half]


def other_sums(came_ref, heads):
    terms = [came_ref[i] for i in range(heads, came_ref.shape[0])]
    return from_terms(jnp.concatenate(terms, axis=0), heads)


def sums_by_head(decay):
    ones = jnp.ones((decay.shape[1], SIZE), F32)
    return jnp.dot(decay, ones, precision=lax.Precision.HIGHEST, preferred_element_type=F32)


def in_terms(total):
    high = total.astype(BF16).astype(F32)
    mid = (total - high).astype(BF16).astype(F32)
    return jnp.concatenate([high, mid, total - high - mid, jnp.zeros_like(total)], axis=0).astype(BF16)


def from_terms(terms, n):
    terms = terms.astype(F32)
    return terms[:n] + terms[n : 2 * n] + terms[2 * n : 3 * n]


def chip_kernel(x_ref, c_ref, sums_ref, keep_ref, came_ref, *refs):
    outs, (gain_ref, both_ref) = refs[:N_X], refs[N_X:]
    heads = sums_ref.shape[0] // N_X
    half = SIZE // 2
    mine = sums_ref[...]
    other = other_sums(came_ref, sums_ref.shape[0])
    first = c_ref[0] == 0
    gain = jnp.exp(jnp.where(first, other, mine))
    gain_ref[0] = jnp.where(first, gain, 1.0)
    gain_ref[1] = jnp.where(first, 1.0, gain)
    both_ref[...] = mine + other
    for k, out in enumerate(outs):
        head = lax.rem(x_ref[0] + offset(k, c_ref[0]), N_X) * heads
        for h in range(heads):
            row = pl.ds(head + h, 1)
            state = (
                keep_ref[head + h].astype(F32) * gain_ref[0, row, :]
                + came_ref[head + h].astype(F32) * gain_ref[1, row, :]
            )
            out[h * half : (h + 1) * half, :] = state.astype(BF16)
        out[heads * half :, :] = in_terms(both_ref[pl.ds(pl.multiple_of(head, heads), heads), :])


def group_kernel(x_ref, c_ref, *refs):
    came, (out, order) = refs[:N_X], refs[N_X:]
    rows = out.shape[0]
    half = SIZE // 2
    heads = rows // (half + 4)
    for k, ref in enumerate(came):
        order[lax.rem(x_ref[0] - offset(k, c_ref[0]) + N_X, N_X)] = ref[...]
    sums = [from_terms(order[p, heads * half :, :], heads) for p in range(N_X)]
    gains = [jnp.exp(a) for a in sums]
    for h in range(heads):
        span = slice(h * half, (h + 1) * half)
        state = order[0, span, :].astype(F32)
        for p in range(1, N_X):
            state = state * gains[p][h : h + 1] + order[p, span, :].astype(F32)
        out[span, :] = state.astype(BF16)
    out[heads * half :, :] = in_terms(sum(sums[1:], sums[0]))


def enter_kernel(x_ref, z_ref, c_ref, order, *refs):
    groups, outs, states = refs[: N_Z - 1], refs[N_Z - 1 : -1], refs[-1]
    rows = order.shape[1]
    half = SIZE // 2
    heads = rows // (half + 4)
    gains = [jnp.exp(from_terms(ref[heads * half :, :], heads)) for ref in groups]
    steps = [jnp.exp(from_terms(order[p, heads * half :, :], heads)) for p in range(N_X)]
    for h in range(heads):
        span = slice(h * half, (h + 1) * half)
        head = slice(h, h + 1)
        state = jnp.zeros((half, SIZE), F32)
        for i, ref in enumerate(groups):
            after = state * gains[i][head] + ref[span, :].astype(F32)
            state = jnp.where(z_ref[0] >= N_Z - 1 - i, after, 0.0)
        for p in range(N_X):
            states[p, span, :] = state.astype(BF16)
            state = state * steps[p][head] + order[p, span, :].astype(F32)
    for k, out in enumerate(outs):
        out[...] = states[lax.rem(x_ref[0] - offset(k, c_ref[0]) + N_X, N_X)]


def bridge_kernel(x_ref, c_ref, sums_ref, keep_ref, came_ref, *refs):
    entering, (mine_ref, send_ref, gain_ref) = refs[:N_X], refs[N_X:]
    half = SIZE // 2
    heads = entering[0].shape[0] // half
    first = c_ref[0] == 0
    mine = sums_ref[...]
    other = other_sums(came_ref, sums_ref.shape[0])
    gain_ref[...] = jnp.exp(jnp.where(first, mine, other))
    for k, ref in enumerate(entering):
        head = lax.rem(x_ref[0] + offset(k, c_ref[0]), N_X) * heads
        for h in range(heads):
            state = ref[h * half : (h + 1) * half, :].astype(F32)
            added = jnp.where(first, keep_ref[head + h].astype(F32), came_ref[head + h].astype(F32))
            after = state * gain_ref[pl.ds(head + h, 1), :] + added
            mine_ref[head + h] = jnp.where(first, state, after).astype(BF16)
            send_ref[head + h] = jnp.where(first, after, state).astype(BF16)


def intra_kernel(q_ref, k_ref, v_ref, decay_ref, out_ref):
    heads, rows = decay_ref.shape
    cum = running_sum(decay_ref[...])
    cum_rows = running_sum_rows(decay_ref[...])
    t = lax.broadcasted_iota(jnp.int32, (rows, rows), 0)
    s = lax.broadcasted_iota(jnp.int32, (rows, rows), 1)
    causal = s <= t
    for h in range(heads):
        cols = slice(h * SIZE, (h + 1) * SIZE)
        score = lax.dot_general(
            q_ref[:, cols], k_ref[:, cols], (((1,), (1,)), ((), ())), preferred_element_type=F32
        )
        diff = jnp.where(causal, cum[:, h : h + 1] - cum_rows[h : h + 1, :], 0.0)
        weight = jnp.where(causal, score * jnp.exp(diff), 0.0).astype(BF16)
        out_ref[:, cols] = jnp.dot(weight, v_ref[:, cols], preferred_element_type=F32)


def final_kernel(
    c_ref, q_ref, intra_ref, mine_ref, came_ref, decay_ref, gain_ref, out_ref, total_ref, state_ref
):
    heads, rows = decay_ref.shape
    half = SIZE // 2
    grown = jnp.exp(running_sum(decay_ref[...]))
    square = jnp.zeros((rows, SIZE), F32)
    mine = pl.ds(pl.multiple_of(c_ref[0] * half, half), half)
    other = pl.ds(pl.multiple_of((1 - c_ref[0]) * half, half), half)
    state_ref[:, mine, :] = mine_ref[...]
    state_ref[:, other, :] = came_ref[...]
    for h in range(heads):
        cols = slice(h * SIZE, (h + 1) * SIZE)
        cross = jnp.dot(q_ref[:, cols], state_ref[h], preferred_element_type=F32)
        total = intra_ref[:, cols] + grown[:, h : h + 1] * cross
        total_ref[:, cols] = total
        square += total * total
    mean = jnp.sum(square, axis=1, keepdims=True) / (heads * SIZE)
    scale = lax.rsqrt(mean + 1e-06)
    for h in range(heads):
        cols = slice(h * SIZE, (h + 1) * SIZE)
        out_ref[:, cols] = (total_ref[:, cols] * scale * gain_ref[:, cols]).astype(BF16)


LOG2E = 1.4426950408889634
SCALE = LOG2E / SIZE**0.5
N_Z, N_X = 8, 4
HIDDEN = -1e30


def call(kernel, outs, scalars, arrays, scratch=()):
    name = getattr(kernel, "func", kernel).__name__
    return pl.pallas_call(
        kernel,
        name=name,
        out_shape=outs,
        in_specs=[pl.BlockSpec(memory_space=pltpu.SMEM)] * len(scalars)
        + [pl.BlockSpec(memory_space=pltpu.VMEM)] * len(arrays),
        scratch_shapes=list(scratch),
        compiler_params=params(),
    )(*scalars, *arrays)


def shape(rows, cols, dtype=BF16):
    return jax.ShapeDtypeStruct((rows, cols), dtype)


def offset(k, core):
    one = jnp.where(core == 0, 1, N_X - 1)
    return (0, N_X // 2, one, N_X - one)[k]


def pack_kernel(x_ref, c_ref, q_ref, k_ref, v_ref, *outs):
    wide = q_ref.shape[1] // N_X
    for k, out in enumerate(outs):
        j = lax.rem(x_ref[0] + offset(k, c_ref[0]), N_X)
        out[:, :wide] = q_ref[:, pl.ds(pl.multiple_of(j * wide, wide), wide)]
        head = pl.ds(pl.multiple_of(j * SIZE, SIZE), SIZE)
        out[:, wide : wide + SIZE] = k_ref[:, head]
        out[:, wide + SIZE :] = v_ref[:, head]


def stack_kernel(*refs):
    came, out = refs[:N_X], refs[N_X]
    tokens = came[0].shape[0]
    for k, ref in enumerate(came):
        out[k * tokens : (k + 1) * tokens, :] = ref[...]


def chunk_kernel(c_ref, mine_ref, other_ref, out_ref):
    rows, wide = mine_ref.shape
    out_ref[pl.ds(pl.multiple_of(c_ref[0] * rows, rows), rows), :] = mine_ref[:, wide - 2 * SIZE :]
    out_ref[pl.ds(pl.multiple_of((1 - c_ref[0]) * rows, rows), rows), :] = other_ref[:, wide - 2 * SIZE :]


def group_positions(x, core, shape, axis, tokens):
    i = lax.broadcasted_iota(jnp.int32, shape, axis)
    part = lax.div(i, N_X * tokens)
    k = lax.rem(lax.div(i, tokens), N_X)
    from_core = jnp.where(part == 0, core, 1 - core)
    away = jnp.zeros_like(k)
    for n in range(1, N_X):
        away = jnp.where(k == n, offset(n, from_core), away)
    from_x = lax.rem(x - away + N_X, N_X)
    return (2 * from_x + from_core) * tokens + lax.rem(i, tokens)


def own_kernel(x_ref, c_ref, mine_ref, other_ref, q_ref, top_ref, norm_ref, accum_ref):
    part, wide = mine_ref.shape
    tokens = part // N_X
    heads = wide // SIZE - 2
    key_pos = group_positions(x_ref[0], c_ref[0], (part, 1), 0, tokens)
    q_pos = group_positions(x_ref[0], c_ref[0], (1, 2 * part), 1, tokens)
    seen = key_pos <= q_pos
    k = mine_ref[:, wide - 2 * SIZE : wide - SIZE]
    v = mine_ref[:, wide - SIZE :]
    for h in range(heads):
        cols = slice(h * SIZE, (h + 1) * SIZE)
        q = jnp.concatenate([mine_ref[:, cols], other_ref[:, cols]], axis=0)
        q_ref[h] = q
        s = lax.dot_general(k, q, (((1,), (1,)), ((), ())), preferred_element_type=F32)
        s = jnp.where(seen, s * SCALE, HIDDEN)
        top = jnp.max(s, axis=0, keepdims=True)
        p = jnp.exp2(s - top)
        top_ref[h] = top
        norm_ref[h] = jnp.sum(p, axis=0, keepdims=True)
        accum_ref[h] = lax.dot_general(
            v, p.astype(BF16), (((0,), (0,)), ((), ())), preferred_element_type=F32
        )


def visit(q, top, norm, accum, k, v, seen):
    s = lax.dot_general(k, q, (((1,), (1,)), ((), ())), preferred_element_type=F32) * SCALE
    here = jnp.max(s, axis=0, keepdims=True)
    new_top = jnp.maximum(top, jnp.where(seen, here, HIDDEN))
    shrink = jnp.exp2(top - new_top)
    p = jnp.exp2(s - jnp.where(seen, new_top, -2.0 * HIDDEN))
    norm = norm * shrink + jnp.sum(p, axis=0, keepdims=True)
    accum = accum * shrink + lax.dot_general(
        v, p.astype(BF16), (((0,), (0,)), ((), ())), preferred_element_type=F32
    )
    return new_top, norm, accum


def more_kernel(step, z_ref, c_ref, q_ref, top_ref, norm_ref, accum_ref, chunk_ref, *outs):
    new_top, new_norm, new_accum = outs
    seen = z_ref[0] >= jnp.where(c_ref[0] == 0, step, N_Z - step)
    k, v = chunk_ref[:, :SIZE], chunk_ref[:, SIZE:]
    for h in range(q_ref.shape[0]):
        new_top[h], new_norm[h], new_accum[h] = visit(
            q_ref[h], top_ref[h], norm_ref[h], accum_ref[h], k, v, seen
        )


def last_kernel(z_ref, c_ref, q_ref, top_ref, norm_ref, accum_ref, chunk_ref, mine_ref, send_ref):
    part = mine_ref.shape[2]

    def put(h, top, norm, accum):
        for out, span in ((mine_ref, slice(0, part)), (send_ref, slice(part, 2 * part))):
            out[h, :SIZE, :] = accum[:, span]
            out[h, SIZE : SIZE + 1, :] = norm[:, span]
            out[h, SIZE + 1 : SIZE + 2, :] = top[:, span]

    @pl.when(c_ref[0] == 0)
    def _():
        for h in range(q_ref.shape[0]):
            put(h, top_ref[h], norm_ref[h], accum_ref[h])

    @pl.when(c_ref[0] == 1)
    def _():
        k, v = chunk_ref[:, :SIZE], chunk_ref[:, SIZE:]
        for h in range(q_ref.shape[0]):
            seen = z_ref[0] >= N_Z // 2
            put(h, *visit(q_ref[h], top_ref[h], norm_ref[h], accum_ref[h], k, v, seen))


def join_kernel(mine_ref, came_ref, *outs):
    tokens = outs[0].shape[0]
    for h in range(mine_ref.shape[0]):
        tops = [ref[h, SIZE + 1 : SIZE + 2, :] for ref in (mine_ref, came_ref)]
        top = jnp.maximum(*tops)
        one, two = (jnp.exp2(t - top) for t in tops)
        norm = mine_ref[h, SIZE : SIZE + 1, :] * one + came_ref[h, SIZE : SIZE + 1, :] * two
        accum = mine_ref[h, :SIZE, :] * (one / norm) + came_ref[h, :SIZE, :] * (two / norm)
        out = jnp.transpose(accum).astype(BF16)
        for k, ref in enumerate(outs):
            ref[:, h * SIZE : (h + 1) * SIZE] = out[k * tokens : (k + 1) * tokens]


def place_kernel(x_ref, c_ref, *refs):
    came, out = refs[:N_X], refs[N_X]
    wide = came[0].shape[1]
    for k, ref in enumerate(came):
        j = lax.rem(x_ref[0] + offset(k, c_ref[0]), N_X)
        out[:, pl.ds(pl.multiple_of(j * wide, wide), wide)] = ref[...]


def along_x(a, way):
    steps = (way, -way)
    pairs = [(2 * i + c, 2 * ((i + steps[c]) % N_X) + c) for i in range(N_X) for c in range(2)]
    return lax.ppermute(a, ("x", "core"), pairs)


def to_partners(parts):
    own, opposite, near, far = parts
    return [own, along_x(along_x(opposite, 1), 1), along_x(near, 1), along_x(far, -1)]


def from_partners(parts):
    own, opposite, near, far = parts
    return [own, along_x(opposite, 2), along_x(near, -1), along_x(far, 1)]


def along_z(a, k):
    return lax.ppermute(a, "z", [(i, (i + k) % N_Z) for i in range(N_Z)])


def along_ring(a):
    pairs = [(2 * i + c, 2 * ((i + (1, -1)[c]) % N_Z) + c) for i in range(N_Z) for c in range(2)]
    return lax.ppermute(a, ("z", "core"), pairs)


def other_core(a):
    return lax.ppermute(a, "core", [(0, 1), (1, 0)])


def after(a, *others):
    return lax.optimization_barrier((a, others))[0]


def attention_layers(lin_q, lin_k, lin_v, log_decay, norm_gain, soft_q, soft_k, soft_v):
    tokens, lin_heads = log_decay.shape
    decay = log_decay.T
    rows_half = SIZE // 2
    lin_share = lin_heads // N_X
    wide = soft_q.shape[1] // N_X
    heads = wide // SIZE
    part = N_X * tokens
    z, x, core = (lax.axis_index(a).astype(jnp.int32).reshape(1) for a in ("z", "x", "core"))
    packed = call(pack_kernel, (shape(tokens, wide + 2 * SIZE),) * N_X, (x, core), (soft_q, soft_k, soft_v))
    keep, send, decay_sums = call(
        contrib_kernel,
        (
            jax.ShapeDtypeStruct((lin_heads, rows_half, SIZE), BF16),
            jax.ShapeDtypeStruct((lin_heads + 4 * lin_heads // rows_half, rows_half, SIZE), BF16),
            jax.ShapeDtypeStruct((lin_heads, SIZE), F32),
        ),
        (core,),
        (lin_k, lin_v, decay),
    )
    state_came = other_core(send)
    of_chip = shape(lin_share * (rows_half + 4), SIZE)
    parts = call(
        chip_kernel,
        (of_chip,) * N_X,
        (x, core),
        (decay_sums, keep, state_came),
        [pltpu.VMEM((2, lin_heads, SIZE), F32), pltpu.VMEM((lin_heads, SIZE), F32)],
    )
    intra = call(
        intra_kernel, shape(tokens, lin_heads * SIZE, F32), (), (lin_q, lin_k, lin_v, decay)
    )
    packed = after(packed, parts[0])
    soft_came = to_partners(packed)
    parts_came = to_partners(parts)
    group, order = call(
        group_kernel, (of_chip, jax.ShapeDtypeStruct((N_X, *of_chip.shape), BF16)), (x, core), parts_came
    )
    mine = call(stack_kernel, shape(part, wide + 2 * SIZE), (), after(soft_came, group, intra))
    other = other_core(mine)
    chunk = call(chunk_kernel, shape(2 * part, 2 * SIZE), (core,), (mine, other))
    row = jax.ShapeDtypeStruct((heads, 1, 2 * part), F32)
    held_shape = (row, row, jax.ShapeDtypeStruct((heads, SIZE, 2 * part), F32))
    state_up, state_down, groups = group, group, {}
    for step in range(1, N_Z // 2 + 1):
        state_up = along_z(state_up, 1)
        groups[step] = state_up
        if step < N_Z // 2:
            state_down = along_z(state_down, -1)
            groups[N_Z - step] = state_down
    states = call(
        enter_kernel,
        (shape(lin_share * rows_half, SIZE),) * N_X,
        (x, z, core),
        [order] + [groups[d] for d in range(N_Z - 1, 0, -1)],
        [pltpu.VMEM((N_X, lin_share * rows_half, SIZE), BF16)],
    )
    states = from_partners(states)
    for step in range(1, N_Z // 2 + 1):
        came = along_ring(chunk)
        if step == 1:
            q, *held = call(
                own_kernel,
                (jax.ShapeDtypeStruct((heads, 2 * part, SIZE), BF16), *held_shape),
                (x, core),
                (mine, other),
            )
        else:
            held = call(
                functools.partial(more_kernel, step - 1), held_shape, (z, core), (q, *held, chunk)
            )
        if step < N_Z // 2 - 1:
            ahead = [groups[step + 1]] + ([groups[N_Z - step - 1]] if step + 1 < N_Z // 2 else [])
        else:
            ahead = [] if step < N_Z // 2 else states[1:]
        chunk = after(came, held[0], *ahead)
    sums = jax.ShapeDtypeStruct((heads, SIZE + 8, part), F32)
    sums_mine, sums_send = call(last_kernel, (sums, sums), (z, core), (q, *held, chunk))
    outs = call(
        join_kernel, (shape(tokens, wide),) * N_X, (), (sums_mine, other_core(sums_send))
    )
    outs = from_partners(outs)
    halves = jax.ShapeDtypeStruct((lin_heads, rows_half, SIZE), BF16)
    mine, send = call(
        bridge_kernel,
        (halves, halves),
        (x, core),
        [decay_sums, keep, state_came, *states],
        [pltpu.VMEM((lin_heads, SIZE), F32)],
    )
    lin_out = call(
        final_kernel,
        shape(tokens, lin_heads * SIZE),
        (core,),
        (lin_q, intra, mine, other_core(send), decay, norm_gain.reshape(1, -1)),
        [pltpu.VMEM(lin_q.shape, F32), pltpu.VMEM((lin_heads, SIZE, SIZE), BF16)],
    )
    soft_out = call(place_kernel, shape(tokens, wide * N_X), (x, core), outs)
    return lin_out, soft_out


def solution(mesh):
    grid = mesh.devices.reshape(mesh.devices.shape[0], N_Z, N_X, 2)
    mesh = jax.sharding.Mesh(grid, ("dp", "z", "x", "core"))
    split = P(("dp", "z", "x", "core"), None)
    in_specs = (split,) * 4 + (P(),) + (split,) * 3
    return jax.shard_map(
        attention_layers, mesh=mesh, in_specs=in_specs, out_specs=(split, split), check_vma=False
    )
```
